32 devices in a mesh: chain: 8 (over z, core), src: 4 (over y, x).
Axes of the slice: x: 2, y: 2, z: 4, core: 2. Of those that a mesh axis runs over, the one named last changes fastest.
Arguments:
- sources: bfloat16 [256, 4096], P('src', 'chain'), may hold values from -6 to 6
- forward: bfloat16 [256, 4096], P('src', 'chain')
- inv_diag: bfloat16 [8, 512, 512], P('chain'), as said below
- coupling: bfloat16 [8, 2, 512, 512], P('chain'), may hold values from -0.5 to 0.5
- pattern: int32 [8, 2], P('chain'), may hold values 0 or 1
Outputs:
- adjoint: bfloat16 [256, 4096], P('src', 'chain')
- direction: float32 [4096], P('chain')
The draws below stay inside these ranges and needn't reach their ends.
Inputs may be any that keep to these rules, and one draw needn't show every extreme that they name: inv_diag is the identity plus a dense perturbation of spectral size about one.
All inputs are finite; a program needn't handle non-finite values. No bound on the sum of `pattern` on one device may be relied on, other than what follows from the above.
Results may differ from the reference program's by a relative error of at most 0.02.
Values may be sent and summed in bfloat16 or wider, within the bound.
A program may use at most 64 MiB of HBM per device.

```python
import jax
import jax.numpy as jnp
from jax import lax

B = 512
SRC_DEV = 64
NP = 8
NCELL = 4096
TOTAL_SRC = 256


def draw_inv_diag(key, part):
    spread = jax.random.normal(key, (NP, B, B), jnp.float32)
    spread = jnp.clip(spread, -6.0, 6.0) * (0.5 / B ** 0.5)
    return (jnp.eye(B, dtype=jnp.float32)[None] + spread).astype(jnp.bfloat16)


def draw_forward(key, part):
    key_values, key_cols = jax.random.split(key, 2)
    groups = TOTAL_SRC // SRC_DEV
    group_index = jnp.arange(TOTAL_SRC, dtype=jnp.float32)[:, None] // SRC_DEV
    row_scale = 3.0 ** (group_index / max(groups - 1, 1)) * 0.5
    col_scale = 10.0 ** jax.random.uniform(key_cols, (1, NCELL), jnp.float32, -0.5, 0.5)
    values = jnp.clip(jax.random.normal(key_values, (TOTAL_SRC, NCELL), jnp.float32), -4.0, 4.0)
    return (values * row_scale * col_scale).astype(jnp.bfloat16)


def set_ends(entries, key, smallest, high):
    longest = entries.shape.index(max(entries.shape))
    spots = []
    for shift in (0, 1):
        where = [jax.random.randint(jax.random.fold_in(key, axis), (), 0, length) for axis, length in enumerate(entries.shape)]
        where[longest] = (where[longest] + shift) % entries.shape[longest]
        spots.append(tuple(where))
    return entries.at[spots[0]].set(smallest).at[spots[1]].set(high)


def steps_of(rng, shape, cuts, smallest, high):
    factor_of = 1.0
    for axis_at, blocks in cuts:
        steps = jax.random.uniform(jax.random.fold_in(jax.random.fold_in(rng, 6), axis_at), (blocks,), jnp.float32, smallest / len(cuts), high / len(cuts))
        factor_of = factor_of * jnp.repeat(jnp.exp(steps), shape[axis_at] // blocks).reshape((-1,) + (1,) * (len(shape) - 1 - axis_at))
    return factor_of


def centred(rng, dims, scale, bound, cuts=(), held_as=jnp.bfloat16):
    gain = steps_of(rng, dims, cuts, -0.22, 0.18) if cuts else 1.0
    result = jax.random.normal(rng, dims, jnp.float32) * scale * gain
    return jnp.minimum(jnp.maximum(result, -bound), bound).astype(held_as)


def setup_inputs(seed: int = 0) -> dict:
    splits = jax.random.split(jax.random.key(seed), 6)
    return {
        "sources": centred(splits[0], (TOTAL_SRC, NCELL), 1.0, 6.0, ((0, 4), (1, 8))),
        "forward": draw_forward(jax.random.fold_in(splits[5], 71), 0),
        "inv_diag": draw_inv_diag(jax.random.fold_in(splits[5], 71), 0),
        "coupling": centred(splits[3], (NP, 2, B, B), (0.75 / B ** 0.5), 0.5, ((0, 8),)),
        "pattern": set_ends((jax.random.randint(splits[4], (NP, 2), 0, 3) < 2).astype(jnp.int32), jax.random.fold_in(splits[4], 1), 0, 1),
    }


def reference(sources, forward, inv_diag, coupling, pattern):
    empty = jnp.zeros((TOTAL_SRC, B), jnp.bfloat16)
    solved = [empty for panel in range(NP + 2)]
    for panel in reversed(range(NP)):
        rows = sources[:, panel * B:(panel + 1) * B].astype(jnp.float32)
        first = jnp.dot(solved[panel + 1], coupling[panel, 0], preferred_element_type=jnp.float32)
        second = jnp.dot(solved[panel + 2], coupling[panel, 1], preferred_element_type=jnp.float32)
        rows = rows - pattern[panel, 0].astype(jnp.float32) * first - pattern[panel, 1].astype(jnp.float32) * second
        solved[panel] = jnp.dot(rows.astype(jnp.bfloat16), inv_diag[panel], preferred_element_type=jnp.float32).astype(jnp.bfloat16)
    adjoint = jnp.concatenate(solved[:NP], axis=1)
    grad = lax.optimization_barrier(jnp.sum(forward.astype(jnp.float32) * adjoint.astype(jnp.float32), axis=0))
    scale = jnp.sqrt(jnp.mean(grad * grad) + 1e-06)
    return (adjoint, grad / scale)
```

```python
import functools

import jax
import jax.numpy as jnp
from jax import lax
from jax.experimental import pallas as pl
from jax.experimental.pallas import tpu as pltpu
from jax.sharding import PartitionSpec as P

F32 = jnp.float32
BF16 = jnp.bfloat16
MESH = pl.DeviceIdType.MESH


def matmul(a, b):
    return jnp.dot(a, b, preferred_element_type=F32)


def kernel(n, groups, pattern, sources, forward, inv_diag, coupling, adjoint, direction,
           rows, waves, inv, blocks, base, near_mat, far_mat, near, far, solved, parts, squares,
           load_sem, store_sem, send_sem, near_sem, far_sem, part_send, part_recv, sq_send, sq_recv):
    k = lax.axis_index("chain")
    g = lax.axis_index("src")
    odd = lax.rem(k, 2) == 1

    loads = [
        pltpu.make_async_copy(inv_diag.at[0], inv, load_sem.at[0]),
        pltpu.make_async_copy(sources, rows, load_sem.at[1]),
        pltpu.make_async_copy(coupling.at[0, 0], blocks.at[0], load_sem.at[2]),
        pltpu.make_async_copy(coupling.at[0, 1], blocks.at[1], load_sem.at[3]),
        pltpu.make_async_copy(forward, waves, load_sem.at[4]),
    ]
    for load in loads:
        load.start()

    barrier = pltpu.get_barrier_semaphore()
    for step in range(1, n):
        pl.semaphore_signal(barrier, inc=1, device_id=(lax.rem(k + step, n), g), device_id_type=MESH)
    for step in range(1, groups):
        pl.semaphore_signal(barrier, inc=1, device_id=(k, lax.rem(g + step, groups)), device_id_type=MESH)

    def remote(src, dst, send, recv, chain_to, src_to):
        return pltpu.make_async_remote_copy(
            src_ref=src, dst_ref=dst, send_sem=send, recv_sem=recv,
            device_id=(chain_to, src_to), device_id_type=MESH,
        )

    one_down = lax.max(k - 1, 0)
    two_down = lax.max(k - 2, 0)
    to_near = remote(solved, near, send_sem.at[0], near_sem, one_down, g)
    to_far = remote(solved, far, send_sem.at[1], far_sem, two_down, g)
    onward = remote(near, far, send_sem.at[2], far_sem, one_down, g)

    loads[0].wait()
    loads[1].wait()
    base[...] = matmul(rows[...], inv[...])
    pl.semaphore_wait(barrier, n - 1 + groups - 1)

    loads[2].wait()
    loads[3].wait()

    @pl.when(k < n - 1)
    def _():
        near_mat[...] = (matmul(blocks[0], inv[...]) * -pattern[0, 0].astype(F32)).astype(BF16)

    @pl.when(k < n - 2)
    def _():
        far_mat[...] = (matmul(blocks[1], inv[...]) * -pattern[0, 1].astype(F32)).astype(BF16)
        to_far.wait_recv()
        base[...] += matmul(far[...], far_mat[...])

    @pl.when(k < n - 1)
    def _():
        to_near.wait_recv()

        @pl.when(odd)
        def _():
            onward.start()

        solved[...] = (base[...] + matmul(near[...], near_mat[...])).astype(BF16)

    @pl.when(k == n - 1)
    def _():
        solved[...] = base[...].astype(BF16)

    @pl.when(k > 0)
    def _():
        to_near.start()

    @pl.when(odd & (k > 1))
    def _():
        to_far.start()

    store = pltpu.make_async_copy(solved, adjoint, store_sem)
    store.start()

    loads[4].wait()
    parts[g] = jnp.sum(waves[...].astype(F32) * solved[...].astype(F32), axis=0, keepdims=True)

    def part_copy(step, owner):
        return remote(parts.at[owner], parts.at[owner], part_send.at[step], part_recv.at[owner],
                      k, lax.rem(g + step, groups))

    for step in range(1, groups):
        part_copy(step, g).start()
    for step in range(1, groups):
        part_copy(step, lax.rem(g + groups - step, groups)).wait_recv()
    grad = parts[0]
    for group in range(1, groups):
        grad = grad + parts[group]
    squares[k] = jnp.broadcast_to(jnp.sum(grad * grad, axis=1, keepdims=True), (1, 128))

    def square_copy(step, owner):
        return remote(squares.at[owner], squares.at[owner], sq_send.at[step], sq_recv.at[owner],
                      lax.rem(k + step, n), g)

    for step in range(1, n):
        square_copy(step, k).start()
    for step in range(1, n):
        square_copy(step, lax.rem(k + n - step, n)).wait_recv()
    total = squares[0]
    for panel in range(1, n):
        total = total + squares[panel]
    count = float(n * grad.shape[1])
    scale = jnp.sqrt(total / count + 1e-06)
    direction[...] = grad / jnp.broadcast_to(scale[:, :1], grad.shape)

    for step in range(1, groups):
        part_copy(step, g).wait_send()
    for step in range(1, n):
        square_copy(step, k).wait_send()

    @pl.when(k > 0)
    def _():
        to_near.wait_send()

    @pl.when(odd & (k > 1))
    def _():
        to_far.wait_send()

    @pl.when(odd & (k < n - 1))
    def _():
        onward.wait_send()

    store.wait()


def solution(mesh):
    n = mesh.shape["chain"]
    groups = mesh.shape["src"]

    def per_device(sources, forward, inv_diag, coupling, pattern):
        count, width = sources.shape
        anywhere = pl.BlockSpec(memory_space=pl.ANY)
        adjoint, direction = pl.pallas_call(
            functools.partial(kernel, n, groups),
            out_shape=(
                jax.ShapeDtypeStruct((count, width), BF16),
                jax.ShapeDtypeStruct((1, width), F32),
            ),
            in_specs=[pl.BlockSpec(memory_space=pltpu.SMEM)] + [anywhere] * 4,
            out_specs=(anywhere, pl.BlockSpec(memory_space=pltpu.VMEM)),
            scratch_shapes=[
                pltpu.VMEM((count, width), BF16),
                pltpu.VMEM((count, width), BF16),
                pltpu.VMEM((width, width), BF16),
                pltpu.VMEM((2, width, width), BF16),
                pltpu.VMEM((count, width), F32),
                pltpu.VMEM((width, width), BF16),
                pltpu.VMEM((width, width), BF16),
                pltpu.VMEM((count, width), BF16),
                pltpu.VMEM((count, width), BF16),
                pltpu.VMEM((count, width), BF16),
                pltpu.VMEM((groups, 1, width), F32),
                pltpu.VMEM((n, 1, 128), F32),
                pltpu.SemaphoreType.DMA((5,)),
                pltpu.SemaphoreType.DMA,
                pltpu.SemaphoreType.DMA((3,)),
                pltpu.SemaphoreType.DMA,
                pltpu.SemaphoreType.DMA,
                pltpu.SemaphoreType.DMA((groups,)),
                pltpu.SemaphoreType.DMA((groups,)),
                pltpu.SemaphoreType.DMA((n,)),
                pltpu.SemaphoreType.DMA((n,)),
            ],
            compiler_params=pltpu.CompilerParams(
                collective_id=0, has_side_effects=True, vmem_limit_bytes=60 * 1024 * 1024
            ),
            cost_estimate=pl.CostEstimate(
                flops=2 * width * width * (2 * width + 3 * count),
                bytes_accessed=6 * width * width + 6 * count * width,
                transcendentals=0,
            ),
        )(pattern, sources, forward, inv_diag, coupling)
        return adjoint, direction.reshape(width)

    return jax.shard_map(
        per_device,
        mesh=mesh,
        in_specs=(
            P("src", "chain"),
            P("src", "chain"),
            P("chain", None, None),
            P("chain", None, None, None),
            P("chain", None),
        ),
        out_specs=(P("src", "chain"), P("chain")),
        check_vma=False,
    )
```

```python
import functools

import jax
import jax.numpy as jnp
from jax import lax
from jax.experimental import pallas as pl
from jax.experimental.pallas import tpu as pltpu
from jax.sharding import PartitionSpec as P

F32 = jnp.float32
BF16 = jnp.bfloat16
MESH = pl.DeviceIdType.MESH


def matmul(a, b):
    return jnp.dot(a, b, preferred_element_type=F32)


def kernel(n, groups, pattern, sources, forward, inv_diag, coupling, adjoint, direction,
           rows, waves, inv, blocks, base, mats, above, solved, mine_part, parts, squares,
           load_sem, store_sem, pair_send, pair_recv, down_send, down_recv, back_send, back_recv,
           part_send, part_recv, sq_send, sq_recv):
    k = lax.axis_index("chain")
    g = lax.axis_index("src")
    c = lax.rem(k, 2)
    first = k - c
    peer = first + 1 - c
    top = k >= n - 2
    bottom = k < 2
    half = rows.shape[0] // 2
    mine = pl.ds(pl.multiple_of(c * half, half), half)
    theirs = pl.ds(pl.multiple_of((1 - c) * half, half), half)

    loads = [
        pltpu.make_async_copy(inv_diag.at[0], inv, load_sem.at[0]),
        pltpu.make_async_copy(sources, rows, load_sem.at[1]),
        pltpu.make_async_copy(coupling.at[0, 0], blocks.at[0], load_sem.at[2]),
        pltpu.make_async_copy(coupling.at[0, 1], blocks.at[1], load_sem.at[3]),
        pltpu.make_async_copy(forward, waves.at[c], load_sem.at[4]),
    ]
    for i in (0, 1, 3, 2, 4):
        loads[i].start()

    barrier = pltpu.get_barrier_semaphore()
    for step in range(1, n):
        pl.semaphore_signal(barrier, inc=1, device_id=(lax.rem(k + step, n), g), device_id_type=MESH)
    for step in range(1, groups):
        for other in (k, peer):
            pl.semaphore_signal(barrier, inc=1, device_id=(other, lax.rem(g + step, groups)), device_id_type=MESH)

    def remote(src, dst, send, recv, chain_to, src_to):
        return pltpu.make_async_remote_copy(
            src_ref=src, dst_ref=dst, send_sem=send, recv_sem=recv,
            device_id=(chain_to, src_to), device_id_type=MESH,
        )

    def pair(i, ref):
        return remote(ref, ref, pair_send.at[i], pair_recv.at[i], peer, g)

    give_base = pair(0, base.at[c, theirs])
    take_base = pair(0, base.at[1 - c, mine])
    give_mat = [pair(1, mats.at[c, 0]), pair(2, mats.at[c, 1])]
    take_mat = [pair(1, mats.at[1 - c, 0]), pair(2, mats.at[1 - c, 1])]
    give_waves = pair(3, waves.at[c, theirs])
    take_waves = pair(3, waves.at[1 - c, mine])
    give_top = pair(4, solved.at[1])
    give_back = remote(solved.at[1 - c, mine], solved.at[1 - c, mine], back_send, back_recv, peer, g)
    take_back = remote(solved.at[c, theirs], solved.at[c, theirs], back_send, back_recv, peer, g)

    def down(panel):
        return remote(solved.at[panel, mine], above.at[panel], down_send.at[panel], down_recv.at[panel],
                      lax.max(k - 2, 0), g)

    def down_top(panel, core):
        part = pl.ds(core * half, half)
        return remote(solved.at[panel, part], above.at[panel], down_send.at[core], down_recv.at[panel],
                      lax.max(first - 2 + core, 0), g)

    def product(which):
        return (matmul(blocks[which], inv[...]) * -pattern[0, which].astype(F32)).astype(BF16)

    def overlap(panel, part):
        field = waves[panel, part].astype(F32) * solved[panel, part].astype(F32)
        return jnp.sum(field, axis=0, keepdims=True)

    loads[0].wait()
    loads[1].wait()
    base[c] = matmul(rows[...], inv[...])
    pl.semaphore_wait(barrier, n - 1 + 2 * (groups - 1))

    @pl.when(top & (c == 1))
    def _():
        solved[1] = base[1].astype(BF16)
        give_top.start()
        if n > 2:
            for core in range(2):
                down_top(1, core).start()
        loads[2].wait()
        loads[3].wait()
        loads[4].wait()
        mine_part[1] = overlap(1, slice(None))
        mine_part[0] = jnp.zeros_like(mine_part[0])

    @pl.when(top & (c == 0))
    def _():
        loads[2].wait()
        mats[0, 0] = product(0)
        give_top.wait_recv()
        solved[0] = (base[0] + matmul(solved[1], mats[0, 0])).astype(BF16)
        if n > 2:
            for core in range(2):
                down_top(0, core).start()
        loads[3].wait()
        loads[4].wait()
        mine_part[0] = overlap(0, slice(None))
        mine_part[1] = jnp.zeros_like(mine_part[1])

    @pl.when(jnp.logical_not(top))
    def _():
        give_base.start()
        loads[3].wait()
        mats[c, 1] = product(1)
        give_mat[1].start()
        loads[2].wait()
        mats[c, 0] = product(0)
        give_mat[0].start()
        loads[4].wait()
        give_waves.start()

        take_base.wait_recv()
        take_mat[1].wait_recv()
        take_mat[0].wait_recv()
        down(1).wait_recv()
        high = base[1, mine] + matmul(above[1], mats[1, 1])
        down(0).wait_recv()
        high = (high + matmul(above[0], mats[1, 0])).astype(BF16)
        solved[1, mine] = high

        @pl.when(jnp.logical_not(bottom))
        def _():
            down(1).start()

        low = base[0, mine] + matmul(above[0], mats[0, 1])
        solved[0, mine] = (low + matmul(high, mats[0, 0])).astype(BF16)

        @pl.when(jnp.logical_not(bottom))
        def _():
            down(0).start()

        take_waves.wait_recv()
        mine_part[1] = overlap(1, mine)
        mine_part[0] = overlap(0, mine)

    slot = 2 * g + c

    def part_to(step, flip):
        to = lax.rem(c + flip, 2)
        return remote(mine_part.at[to], parts.at[slot], part_send.at[2 * step + flip],
                      part_recv.at[slot], first + to, lax.rem(g + step, groups))

    def part_from(step, flip):
        owner = 2 * lax.rem(g + groups - step, groups) + lax.rem(c + flip, 2)
        return remote(mine_part.at[0], parts.at[owner], part_send.at[2 * step + flip],
                      part_recv.at[owner], peer, g)

    partners = [(step, flip) for step in range(groups) for flip in range(2) if step + flip > 0]
    for step, flip in reversed(partners):
        part_to(step, flip).start()
    parts[slot] = mine_part[c]

    @pl.when(jnp.logical_not(top))
    def _():
        give_back.start()
        take_back.wait_recv()

    store = pltpu.make_async_copy(solved.at[c], adjoint, store_sem)
    store.start()

    for step, flip in partners:
        part_from(step, flip).wait_recv()
    grad = parts[0]
    for i in range(1, 2 * groups):
        grad = grad + parts[i]
    squares[k] = jnp.broadcast_to(jnp.sum(grad * grad, axis=1, keepdims=True), (1, 128))

    def square_copy(step, owner):
        return remote(squares.at[owner], squares.at[owner], sq_send.at[step], sq_recv.at[owner],
                      lax.rem(k + step, n), g)

    for step in range(1, n):
        square_copy(step, k).start()
    for step in range(1, n):
        square_copy(step, lax.rem(k + n - step, n)).wait_recv()
    total = squares[0]
    for panel in range(1, n):
        total = total + squares[panel]
    count = float(n * grad.shape[1])
    scale = jnp.sqrt(total / count + 1e-06)
    direction[...] = grad / jnp.broadcast_to(scale[:, :1], grad.shape)

    for step, flip in partners:
        part_to(step, flip).wait_send()
    for step in range(1, n):
        square_copy(step, k).wait_send()

    @pl.when(top & (c == 1))
    def _():
        give_top.wait_send()

    if n > 2:
        @pl.when(top)
        def _():
            for core in range(2):
                down_top(c, core).wait_send()

    @pl.when(jnp.logical_not(top))
    def _():
        give_base.wait_send()
        give_mat[0].wait_send()
        give_mat[1].wait_send()
        give_waves.wait_send()
        give_back.wait_send()

        @pl.when(jnp.logical_not(bottom))
        def _():
            down(0).wait_send()
            down(1).wait_send()

    store.wait()


def solution(mesh):
    n = mesh.shape["chain"]
    groups = mesh.shape["src"]

    def per_device(sources, forward, inv_diag, coupling, pattern):
        count, width = sources.shape
        anywhere = pl.BlockSpec(memory_space=pl.ANY)
        adjoint, direction = pl.pallas_call(
            functools.partial(kernel, n, groups),
            out_shape=(
                jax.ShapeDtypeStruct((count, width), BF16),
                jax.ShapeDtypeStruct((1, width), F32),
            ),
            in_specs=[pl.BlockSpec(memory_space=pltpu.SMEM)] + [anywhere] * 4,
            out_specs=(anywhere, pl.BlockSpec(memory_space=pltpu.VMEM)),
            scratch_shapes=[
                pltpu.VMEM((count, width), BF16),
                pltpu.VMEM((2, count, width), BF16),
                pltpu.VMEM((width, width), BF16),
                pltpu.VMEM((2, width, width), BF16),
                pltpu.VMEM((2, count, width), F32),
                pltpu.VMEM((2, 2, width, width), BF16),
                pltpu.VMEM((2, count // 2, width), BF16),
                pltpu.VMEM((2, count, width), BF16),
                pltpu.VMEM((2, 1, width), F32),
                pltpu.VMEM((2 * groups, 1, width), F32),
                pltpu.VMEM((n, 1, 128), F32),
                pltpu.SemaphoreType.DMA((5,)),
                pltpu.SemaphoreType.DMA,
                pltpu.SemaphoreType.DMA((5,)),
                pltpu.SemaphoreType.DMA((5,)),
                pltpu.SemaphoreType.DMA((2,)),
                pltpu.SemaphoreType.DMA((2,)),
                pltpu.SemaphoreType.DMA,
                pltpu.SemaphoreType.DMA,
                pltpu.SemaphoreType.DMA((2 * groups,)),
                pltpu.SemaphoreType.DMA((2 * groups,)),
                pltpu.SemaphoreType.DMA((n,)),
                pltpu.SemaphoreType.DMA((n,)),
            ],
            compiler_params=pltpu.CompilerParams(
                collective_id=0, has_side_effects=True, vmem_limit_bytes=60 * 1024 * 1024
            ),
            cost_estimate=pl.CostEstimate(
                flops=2 * width * width * (2 * width + 3 * count),
                bytes_accessed=6 * width * width + 6 * count * width,
                transcendentals=0,
            ),
        )(pattern, sources, forward, inv_diag, coupling)
        return adjoint, direction.reshape(width)

    return jax.shard_map(
        per_device,
        mesh=mesh,
        in_specs=(
            P("src", "chain"),
            P("src", "chain"),
            P("chain", None, None),
            P("chain", None, None, None),
            P("chain", None),
        ),
        out_specs=(P("src", "chain"), P("chain")),
        check_vma=False,
    )
```

```python
import functools

import jax
import jax.numpy as jnp
from jax import lax
from jax.experimental import pallas as pl
from jax.experimental.pallas import tpu as pltpu
from jax.sharding import PartitionSpec as P

F32 = jnp.float32
BF16 = jnp.bfloat16
MESH = pl.DeviceIdType.MESH


def matmul(a, b):
    return jnp.dot(a, b, preferred_element_type=F32)


def kernel(n, groups, pattern, sources, forward, inv_diag, coupling, adjoint, direction,
           rows, waves, inv, blocks, base, mats, above, solved, mine_part, parts, squares,
           load_sem, pair_send, pair_recv, down_send, down_recv, back_send, back_recv,
           part_send, part_recv, sq_send, sq_recv):
    k = lax.axis_index("chain")
    g = lax.axis_index("src")
    c = lax.rem(k, 2)
    first = k - c
    peer = first + 1 - c
    top = k >= n - 2
    bottom = k < 2
    half = rows.shape[0] // 2
    mine = pl.ds(pl.multiple_of(c * half, half), half)
    theirs = pl.ds(pl.multiple_of((1 - c) * half, half), half)

    loads = [
        pltpu.make_async_copy(inv_diag.at[0], inv, load_sem.at[0]),
        pltpu.make_async_copy(sources, rows, load_sem.at[1]),
        pltpu.make_async_copy(coupling.at[0, 0], blocks.at[0], load_sem.at[2]),
        pltpu.make_async_copy(coupling.at[0, 1], blocks.at[1], load_sem.at[3]),
        pltpu.make_async_copy(forward, waves.at[c], load_sem.at[4]),
    ]
    for i in (0, 1, 3, 2, 4):
        loads[i].start()

    barrier = pltpu.get_barrier_semaphore()
    for step in range(1, n):
        pl.semaphore_signal(barrier, inc=1, device_id=(lax.rem(k + step, n), g), device_id_type=MESH)
    for step in range(1, groups):
        for other in (k, peer):
            pl.semaphore_signal(barrier, inc=1, device_id=(other, lax.rem(g + step, groups)), device_id_type=MESH)

    def remote(src, dst, send, recv, chain_to, src_to):
        return pltpu.make_async_remote_copy(
            src_ref=src, dst_ref=dst, send_sem=send, recv_sem=recv,
            device_id=(chain_to, src_to), device_id_type=MESH,
        )

    def pair(i, ref):
        return remote(ref, ref, pair_send.at[i], pair_recv.at[i], peer, g)

    give_base = pair(0, base.at[c, theirs])
    take_base = pair(0, base.at[1 - c, mine])
    give_mat = [pair(1, mats.at[c, 0]), pair(2, mats.at[c, 1])]
    take_mat = [pair(1, mats.at[1 - c, 0]), pair(2, mats.at[1 - c, 1])]
    give_waves = pair(3, waves.at[c, theirs])
    take_waves = pair(3, waves.at[1 - c, mine])
    give_top = pair(4, solved.at[1])
    give_back = remote(solved.at[1 - c, mine], solved.at[1 - c, mine], back_send, back_recv, peer, g)
    take_back = remote(solved.at[c, theirs], solved.at[c, theirs], back_send, back_recv, peer, g)

    def down(panel):
        return remote(solved.at[panel, mine], above.at[panel], down_send.at[panel], down_recv.at[panel],
                      lax.max(k - 2, 0), g)

    def down_top(panel, core):
        part = pl.ds(core * half, half)
        return remote(solved.at[panel, part], above.at[panel], down_send.at[core], down_recv.at[panel],
                      lax.max(first - 2 + core, 0), g)

    def product(which):
        return (matmul(blocks[which], inv[...]) * -pattern[0, which].astype(F32)).astype(BF16)

    def overlap(panel, part):
        field = waves[panel, part].astype(F32) * solved[panel, part].astype(F32)
        return jnp.sum(field, axis=0, keepdims=True)

    loads[0].wait()
    loads[1].wait()
    base[c] = matmul(rows[...], inv[...])
    pl.semaphore_wait(barrier, n - 1 + 2 * (groups - 1))

    @pl.when(top & (c == 1))
    def _():
        solved[1] = base[1].astype(BF16)
        give_top.start()
        if n > 2:
            for core in range(2):
                down_top(1, core).start()
        loads[2].wait()
        loads[3].wait()
        loads[4].wait()
        mine_part[1] = overlap(1, slice(None))
        mine_part[0] = jnp.zeros_like(mine_part[0])

    @pl.when(top & (c == 0))
    def _():
        loads[2].wait()
        mats[0, 0] = product(0)
        give_top.wait_recv()
        solved[0] = (base[0] + matmul(solved[1], mats[0, 0])).astype(BF16)
        if n > 2:
            for core in range(2):
                down_top(0, core).start()
        loads[3].wait()
        loads[4].wait()
        mine_part[0] = overlap(0, slice(None))
        mine_part[1] = jnp.zeros_like(mine_part[1])

    @pl.when(jnp.logical_not(top))
    def _():
        give_base.start()
        loads[3].wait()
        mats[c, 1] = product(1)
        give_mat[1].start()
        loads[2].wait()
        mats[c, 0] = product(0)
        give_mat[0].start()
        loads[4].wait()
        give_waves.start()

        take_base.wait_recv()
        take_mat[1].wait_recv()
        take_mat[0].wait_recv()
        down(1).wait_recv()
        high = base[1, mine] + matmul(above[1], mats[1, 1])
        down(0).wait_recv()
        high = (high + matmul(above[0], mats[1, 0])).astype(BF16)
        solved[1, mine] = high

        @pl.when(jnp.logical_not(bottom))
        def _():
            down(1).start()

        low = base[0, mine] + matmul(above[0], mats[0, 1])
        solved[0, mine] = (low + matmul(high, mats[0, 0])).astype(BF16)

        @pl.when(jnp.logical_not(bottom))
        def _():
            down(0).start()

        take_waves.wait_recv()
        mine_part[1] = overlap(1, mine)
        mine_part[0] = overlap(0, mine)

    slot = 2 * g + c

    def part_to(step, flip):
        to = lax.rem(c + flip, 2)
        return remote(mine_part.at[to], parts.at[slot], part_send.at[2 * step + flip],
                      part_recv.at[slot], first + to, lax.rem(g + step, groups))

    def part_from(step, flip):
        owner = 2 * lax.rem(g + groups - step, groups) + lax.rem(c + flip, 2)
        return remote(mine_part.at[0], parts.at[owner], part_send.at[2 * step + flip],
                      part_recv.at[owner], peer, g)

    partners = [(step, flip) for step in range(groups) for flip in range(2) if step + flip > 0]
    for step, flip in reversed(partners):
        part_to(step, flip).start()
    parts[slot] = mine_part[c]

    @pl.when(jnp.logical_not(top))
    def _():
        give_back.start()
        take_back.wait_recv()

    adjoint[...] = solved[c]

    for step, flip in partners:
        part_from(step, flip).wait_recv()
    grad = parts[0]
    for i in range(1, 2 * groups):
        grad = grad + parts[i]
    squares[k] = jnp.broadcast_to(jnp.sum(grad * grad, axis=1, keepdims=True), (1, 128))

    def square_copy(step, owner):
        return remote(squares.at[owner], squares.at[owner], sq_send.at[step], sq_recv.at[owner],
                      lax.rem(k + step, n), g)

    for step in range(1, n):
        square_copy(step, k).start()
    for step in range(1, n):
        square_copy(step, lax.rem(k + n - step, n)).wait_recv()
    total = squares[0]
    for panel in range(1, n):
        total = total + squares[panel]
    count = float(n * grad.shape[1])
    scale = jnp.sqrt(total / count + 1e-06)
    direction[...] = grad / jnp.broadcast_to(scale[:, :1], grad.shape)

    for step, flip in partners:
        part_to(step, flip).wait_send()
    for step in range(1, n):
        square_copy(step, k).wait_send()

    @pl.when(top & (c == 1))
    def _():
        give_top.wait_send()

    if n > 2:
        @pl.when(top)
        def _():
            for core in range(2):
                down_top(c, core).wait_send()

    @pl.when(jnp.logical_not(top))
    def _():
        give_base.wait_send()
        give_mat[0].wait_send()
        give_mat[1].wait_send()
        give_waves.wait_send()
        give_back.wait_send()

        @pl.when(jnp.logical_not(bottom))
        def _():
            down(0).wait_send()
            down(1).wait_send()


def solution(mesh):
    n = mesh.shape["chain"]
    groups = mesh.shape["src"]

    def per_device(sources, forward, inv_diag, coupling, pattern):
        count, width = sources.shape
        anywhere = pl.BlockSpec(memory_space=pl.ANY)
        adjoint, direction = pl.pallas_call(
            functools.partial(kernel, n, groups),
            out_shape=(
                pltpu.VMEM((count, width), BF16),
                pltpu.VMEM((1, width), F32),
            ),
            in_specs=[pl.BlockSpec(memory_space=pltpu.SMEM)] + [anywhere] * 4,
            out_specs=(pl.BlockSpec(memory_space=pltpu.VMEM),) * 2,
            scratch_shapes=[
                pltpu.VMEM((count, width), BF16),
                pltpu.VMEM((2, count, width), BF16),
                pltpu.VMEM((width, width), BF16),
                pltpu.VMEM((2, width, width), BF16),
                pltpu.VMEM((2, count, width), F32),
                pltpu.VMEM((2, 2, width, width), BF16),
                pltpu.VMEM((2, count // 2, width), BF16),
                pltpu.VMEM((2, count, width), BF16),
                pltpu.VMEM((2, 1, width), F32),
                pltpu.VMEM((2 * groups, 1, width), F32),
                pltpu.VMEM((n, 1, 128), F32),
                pltpu.SemaphoreType.DMA((5,)),
                pltpu.SemaphoreType.DMA((5,)),
                pltpu.SemaphoreType.DMA((5,)),
                pltpu.SemaphoreType.DMA((2,)),
                pltpu.SemaphoreType.DMA((2,)),
                pltpu.SemaphoreType.DMA,
                pltpu.SemaphoreType.DMA,
                pltpu.SemaphoreType.DMA((2 * groups,)),
                pltpu.SemaphoreType.DMA((2 * groups,)),
                pltpu.SemaphoreType.DMA((n,)),
                pltpu.SemaphoreType.DMA((n,)),
            ],
            compiler_params=pltpu.CompilerParams(
                collective_id=0, has_side_effects=True, vmem_limit_bytes=60 * 1024 * 1024
            ),
            cost_estimate=pl.CostEstimate(
                flops=2 * width * width * (2 * width + 3 * count),
                bytes_accessed=6 * width * width + 6 * count * width,
                transcendentals=0,
            ),
        )(pattern, sources, forward, inv_diag, coupling)
        return adjoint, direction.reshape(width)

    return jax.shard_map(
        per_device,
        mesh=mesh,
        in_specs=(
            P("src", "chain"),
            P("src", "chain"),
            P("chain", None, None),
            P("chain", None, None, None),
            P("chain", None),
        ),
        out_specs=(P("src", "chain"), P("chain")),
        check_vma=False,
    )
```

```python
import functools

import jax
import jax.numpy as jnp
from jax import lax
from jax.experimental import pallas as pl
from jax.experimental.pallas import tpu as pltpu
from jax.sharding import PartitionSpec as P

F32 = jnp.float32
BF16 = jnp.bfloat16
MESH = pl.DeviceIdType.MESH


def matmul(a, b):
    return jnp.dot(a, b, preferred_element_type=F32)


def kernel(n, groups, pattern, sources, forward, inv_diag, coupling, adjoint, direction,
           rows, waves, inv, blocks, base, mats, above, solved, mine_part, parts, squares,
           load_sem, pair_send, pair_recv, down_send, down_recv, back_send, back_recv,
           part_send, part_recv, sq_send, sq_recv):
    k = lax.axis_index("chain")
    g = lax.axis_index("src")
    c = lax.rem(k, 2)
    first = k - c
    peer = first + 1 - c
    top = k >= n - 2
    bottom = k < 2
    half = rows.shape[0] // 2
    mine = pl.ds(pl.multiple_of(c * half, half), half)
    theirs = pl.ds(pl.multiple_of((1 - c) * half, half), half)

    loads = [
        pltpu.make_async_copy(inv_diag.at[0], inv, load_sem.at[0]),
        pltpu.make_async_copy(sources, rows, load_sem.at[1]),
        pltpu.make_async_copy(coupling.at[0, 0], blocks.at[0], load_sem.at[2]),
        pltpu.make_async_copy(coupling.at[0, 1], blocks.at[1], load_sem.at[3]),
        pltpu.make_async_copy(forward, waves.at[c], load_sem.at[4]),
    ]
    for i in (0, 1, 3, 2, 4):
        loads[i].start()

    barrier = pltpu.get_barrier_semaphore()
    for step in range(1, n):
        pl.semaphore_signal(barrier, inc=1, device_id=(lax.rem(k + step, n), g), device_id_type=MESH)
    for step in range(1, groups):
        for other in (k, peer):
            pl.semaphore_signal(barrier, inc=1, device_id=(other, lax.rem(g + step, groups)), device_id_type=MESH)

    def remote(src, dst, send, recv, chain_to, src_to):
        return pltpu.make_async_remote_copy(
            src_ref=src, dst_ref=dst, send_sem=send, recv_sem=recv,
            device_id=(chain_to, src_to), device_id_type=MESH,
        )

    def pair(i, ref):
        return remote(ref, ref, pair_send.at[i], pair_recv.at[i], peer, g)

    give_base = pair(0, base.at[c, theirs])
    take_base = pair(0, base.at[1 - c, mine])
    give_mat = [pair(1, mats.at[c, 0]), pair(2, mats.at[c, 1])]
    take_mat = [pair(1, mats.at[1 - c, 0]), pair(2, mats.at[1 - c, 1])]
    give_waves = pair(3, waves.at[c, theirs])
    take_waves = pair(3, waves.at[1 - c, mine])
    give_top = pair(4, solved.at[1])
    give_back = remote(solved.at[1 - c, mine], solved.at[1 - c, mine], back_send, back_recv, peer, g)
    take_back = remote(solved.at[c, theirs], solved.at[c, theirs], back_send, back_recv, peer, g)

    wide = rows.shape[1] // 2
    halves = (pl.ds(0, wide), pl.ds(wide, wide))

    def down(i):
        if i == 0:
            src, dst = solved.at[1, mine], above.at[1]
        else:
            src, dst = solved.at[0, mine, halves[i - 1]], above.at[0, :, halves[i - 1]]
        return remote(src, dst, down_send.at[i], down_recv.at[i], lax.max(k - 2, 0), g)

    def down_top(i, core):
        part = pl.ds(core * half, half)
        if i == 0:
            src, dst, sent = solved.at[1, part], above.at[1], core
        else:
            src, dst = solved.at[0, part, halves[i - 1]], above.at[0, :, halves[i - 1]]
            sent = 2 * (i - 1) + core
        return remote(src, dst, down_send.at[sent], down_recv.at[i], lax.max(first - 2 + core, 0), g)

    def product(which):
        return (matmul(blocks[which], inv[...]) * -pattern[0, which].astype(F32)).astype(BF16)

    def overlap(panel, part):
        field = waves[panel, part].astype(F32) * solved[panel, part].astype(F32)
        return jnp.sum(field, axis=0, keepdims=True)

    loads[0].wait()
    loads[1].wait()
    base[c] = matmul(rows[...], inv[...])
    pl.semaphore_wait(barrier, n - 1 + 2 * (groups - 1))

    @pl.when(top & (c == 1))
    def _():
        solved[1] = base[1].astype(BF16)
        give_top.start()
        if n > 2:
            for core in range(2):
                down_top(0, core).start()
        loads[2].wait()
        loads[3].wait()
        loads[4].wait()
        mine_part[1] = overlap(1, slice(None))
        mine_part[0] = jnp.zeros_like(mine_part[0])

    @pl.when(top & (c == 0))
    def _():
        loads[2].wait()
        mats[0, 0] = product(0)
        give_top.wait_recv()
        for i, cols in enumerate(halves):
            solved[0, :, cols] = (base[0, :, cols] + matmul(solved[1], mats[0, 0, :, cols])).astype(BF16)
            if n > 2:
                for core in range(2):
                    down_top(1 + i, core).start()
        loads[3].wait()
        loads[4].wait()
        mine_part[0] = overlap(0, slice(None))
        mine_part[1] = jnp.zeros_like(mine_part[1])

    @pl.when(jnp.logical_not(top))
    def _():
        give_base.start()
        loads[3].wait()
        mats[c, 1] = product(1)
        give_mat[1].start()
        loads[2].wait()
        mats[c, 0] = product(0)
        give_mat[0].start()
        loads[4].wait()
        give_waves.start()

        take_base.wait_recv()
        take_mat[1].wait_recv()
        take_mat[0].wait_recv()
        take_waves.wait_recv()

    def solve(last):
        down(0).wait_recv()
        high = base[1, mine] + matmul(above[1], mats[1, 1])
        down(1).wait_recv()
        left = above[0, :, halves[0]]
        high = high + matmul(left, mats[1, 0, halves[0]])
        low = base[0, mine] + matmul(left, mats[0, 1, halves[0]])
        down(2).wait_recv()
        right = above[0, :, halves[1]]
        high = (high + matmul(right, mats[1, 0, halves[1]])).astype(BF16)
        solved[1, mine] = high
        if not last:
            down(0).start()
        low = low + matmul(right, mats[0, 1, halves[1]])
        for i, cols in enumerate(halves):
            piece = low[:, i * wide:(i + 1) * wide] + matmul(high, mats[0, 0, :, cols])
            solved[0, mine, cols] = piece.astype(BF16)
            if not last:
                down(1 + i).start()
        mine_part[1] = overlap(1, mine)
        mine_part[0] = overlap(0, mine)

    @pl.when(bottom & jnp.logical_not(top))
    def _():
        solve(True)

    @pl.when(jnp.logical_not(bottom | top))
    def _():
        solve(False)

    slot = 2 * g + c

    def part_to(step, flip):
        to = lax.rem(c + flip, 2)
        return remote(mine_part.at[to], parts.at[slot], part_send.at[2 * step + flip],
                      part_recv.at[slot], first + to, lax.rem(g + step, groups))

    def part_from(step, flip):
        owner = 2 * lax.rem(g + groups - step, groups) + lax.rem(c + flip, 2)
        return remote(mine_part.at[0], parts.at[owner], part_send.at[2 * step + flip],
                      part_recv.at[owner], peer, g)

    partners = [(step, flip) for step in range(groups) for flip in range(2) if step + flip > 0]
    for step, flip in reversed(partners):
        part_to(step, flip).start()
    parts[slot] = mine_part[c]

    @pl.when(jnp.logical_not(top))
    def _():
        give_back.start()
        take_back.wait_recv()

    adjoint[...] = solved[c]

    for step, flip in partners:
        part_from(step, flip).wait_recv()
    grad = parts[0]
    for i in range(1, 2 * groups):
        grad = grad + parts[i]
    squares[k] = jnp.broadcast_to(jnp.sum(grad * grad, axis=1, keepdims=True), (1, 128))

    def square_copy(step, owner):
        return remote(squares.at[owner], squares.at[owner], sq_send.at[step], sq_recv.at[owner],
                      lax.rem(k + step, n), g)

    for step in reversed(range(1, n)):
        square_copy(step, k).start()
    for step in range(1, n):
        square_copy(step, lax.rem(k + n - step, n)).wait_recv()
    total = squares[0]
    for panel in range(1, n):
        total = total + squares[panel]
    count = float(n * grad.shape[1])
    scale = jnp.sqrt(total / count + 1e-06)
    direction[...] = grad / jnp.broadcast_to(scale[:, :1], grad.shape)

    for step, flip in partners:
        part_to(step, flip).wait_send()
    for step in range(1, n):
        square_copy(step, k).wait_send()

    @pl.when(top & (c == 1))
    def _():
        give_top.wait_send()

    if n > 2:
        @pl.when(top & (c == 1))
        def _():
            for core in range(2):
                down_top(0, core).wait_send()

        @pl.when(top & (c == 0))
        def _():
            for core in range(2):
                down_top(1, core).wait_send()
                down_top(2, core).wait_send()

    @pl.when(jnp.logical_not(top))
    def _():
        give_base.wait_send()
        give_mat[0].wait_send()
        give_mat[1].wait_send()
        give_waves.wait_send()
        give_back.wait_send()

        @pl.when(jnp.logical_not(bottom))
        def _():
            for i in range(3):
                down(i).wait_send()


def solution(mesh):
    n = mesh.shape["chain"]
    groups = mesh.shape["src"]

    def per_device(sources, forward, inv_diag, coupling, pattern):
        count, width = sources.shape
        anywhere = pl.BlockSpec(memory_space=pl.ANY)
        adjoint, direction = pl.pallas_call(
            functools.partial(kernel, n, groups),
            out_shape=(
                pltpu.VMEM((count, width), BF16),
                pltpu.VMEM((1, width), F32),
            ),
            in_specs=[pl.BlockSpec(memory_space=pltpu.SMEM)] + [anywhere] * 4,
            out_specs=(pl.BlockSpec(memory_space=pltpu.VMEM),) * 2,
            scratch_shapes=[
                pltpu.VMEM((count, width), BF16),
                pltpu.VMEM((2, count, width), BF16),
                pltpu.VMEM((width, width), BF16),
                pltpu.VMEM((2, width, width), BF16),
                pltpu.VMEM((2, count, width), F32),
                pltpu.VMEM((2, 2, width, width), BF16),
                pltpu.VMEM((2, count // 2, width), BF16),
                pltpu.VMEM((2, count, width), BF16),
                pltpu.VMEM((2, 1, width), F32),
                pltpu.VMEM((2 * groups, 1, width), F32),
                pltpu.VMEM((n, 1, 128), F32),
                pltpu.SemaphoreType.DMA((5,)),
                pltpu.SemaphoreType.DMA((5,)),
                pltpu.SemaphoreType.DMA((5,)),
                pltpu.SemaphoreType.DMA((4,)),
                pltpu.SemaphoreType.DMA((3,)),
                pltpu.SemaphoreType.DMA,
                pltpu.SemaphoreType.DMA,
                pltpu.SemaphoreType.DMA((2 * groups,)),
                pltpu.SemaphoreType.DMA((2 * groups,)),
                pltpu.SemaphoreType.DMA((n,)),
                pltpu.SemaphoreType.DMA((n,)),
            ],
            compiler_params=pltpu.CompilerParams(
                collective_id=0, has_side_effects=True, vmem_limit_bytes=60 * 1024 * 1024
            ),
            cost_estimate=pl.CostEstimate(
                flops=2 * width * width * (2 * width + 3 * count),
                bytes_accessed=6 * width * width + 6 * count * width,
                transcendentals=0,
            ),
        )(pattern, sources, forward, inv_diag, coupling)
        return adjoint, direction.reshape(width)

    return jax.shard_map(
        per_device,
        mesh=mesh,
        in_specs=(
            P("src", "chain"),
            P("src", "chain"),
            P("chain", None, None),
            P("chain", None, None, None),
            P("chain", None),
        ),
        out_specs=(P("src", "chain"), P("chain")),
        check_vma=False,
    )
```

```python
import functools

import jax
import jax.numpy as jnp
from jax import lax
from jax.experimental import pallas as pl
from jax.experimental.pallas import tpu as pltpu
from jax.sharding import PartitionSpec as P

F32 = jnp.float32
BF16 = jnp.bfloat16
MESH = pl.DeviceIdType.MESH


def matmul(a, b):
    return jnp.dot(a, b, preferred_element_type=F32)


def kernel(n, groups, pattern, sources, forward, inv_diag, coupling, adjoint, direction,
           rows, waves, inv, blocks, base, mats, above, whole, solved, mine_part, parts, squares,
           load_sem, pair_send, pair_recv, down_send, down_recv, whole_recv, back_send, back_recv,
           part_send, part_recv, sq_send, sq_recv):
    k = lax.axis_index("chain")
    g = lax.axis_index("src")
    c = lax.rem(k, 2)
    first = k - c
    peer = first + 1 - c
    relay = n >= 6
    top = k >= n - 2
    owner = k >= (n - 4 if relay else n - 2)
    bottom = k < 2
    half = rows.shape[0] // 2
    mine = pl.ds(pl.multiple_of(c * half, half), half)
    theirs = pl.ds(pl.multiple_of((1 - c) * half, half), half)

    loads = [
        pltpu.make_async_copy(inv_diag.at[0], inv, load_sem.at[0]),
        pltpu.make_async_copy(sources, rows, load_sem.at[1]),
        pltpu.make_async_copy(coupling.at[0, 0], blocks.at[0], load_sem.at[2]),
        pltpu.make_async_copy(coupling.at[0, 1], blocks.at[1], load_sem.at[3]),
        pltpu.make_async_copy(forward, waves.at[c], load_sem.at[4]),
    ]
    for i in (0, 1, 3, 2, 4):
        loads[i].start()

    barrier = pltpu.get_barrier_semaphore()
    for step in range(1, n):
        pl.semaphore_signal(barrier, inc=1, device_id=(lax.rem(k + step, n), g), device_id_type=MESH)
    for step in range(1, groups):
        for other in (k, peer):
            pl.semaphore_signal(barrier, inc=1, device_id=(other, lax.rem(g + step, groups)), device_id_type=MESH)

    def remote(src, dst, send, recv, chain_to, src_to):
        return pltpu.make_async_remote_copy(
            src_ref=src, dst_ref=dst, send_sem=send, recv_sem=recv,
            device_id=(chain_to, src_to), device_id_type=MESH,
        )

    def pair(i, ref):
        return remote(ref, ref, pair_send.at[i], pair_recv.at[i], peer, g)

    give_base = pair(0, base.at[c, theirs])
    take_base = pair(0, base.at[1 - c, mine])
    give_mat = [pair(1, mats.at[c, 0]), pair(2, mats.at[c, 1])]
    take_mat = [pair(1, mats.at[1 - c, 0]), pair(2, mats.at[1 - c, 1])]
    give_waves = pair(3, waves.at[c, theirs])
    take_waves = pair(3, waves.at[1 - c, mine])
    give_top = pair(4, solved.at[1])
    give_back = remote(solved.at[1 - c, mine], solved.at[1 - c, mine], back_send, back_recv, peer, g)
    take_back = remote(solved.at[c, theirs], solved.at[c, theirs], back_send, back_recv, peer, g)

    wide = rows.shape[1] // 2
    halves = (pl.ds(0, wide), pl.ds(wide, wide))

    def down(i):
        if i == 0:
            src, dst = solved.at[1, mine], above.at[1]
        else:
            src, dst = solved.at[0, mine, halves[i - 1]], above.at[0, :, halves[i - 1]]
        return remote(src, dst, down_send.at[i], down_recv.at[i], lax.max(k - 2, 0), g)

    def down_top(i, core):
        part = pl.ds(core * half, half)
        if i == 0:
            src, dst, sent = solved.at[1, part], above.at[1], core
        else:
            src, dst = solved.at[0, part, halves[i - 1]], above.at[0, :, halves[i - 1]]
            sent = 2 * (i - 1) + core
        return remote(src, dst, down_send.at[sent], down_recv.at[i], lax.max(first - 2 + core, 0), g)

    def down_whole(i):
        if i == 0:
            src, dst = solved.at[1], whole.at[1]
        else:
            src, dst = solved.at[0, :, halves[i - 1]], whole.at[0, :, halves[i - 1]]
        return remote(src, dst, down_send.at[i], whole_recv.at[i], lax.max(first - 1, 0), g)

    onward = pair(0, whole.at[0])

    def send_down(i):
        if n <= 2:
            return
        if relay:
            @pl.when(top)
            def _():
                down_whole(i).start()

            @pl.when(jnp.logical_not(top))
            def _():
                for core in range(2):
                    down_top(i, core).start()
        else:
            for core in range(2):
                down_top(i, core).start()

    def product(which):
        return (matmul(blocks[which], inv[...]) * -pattern[0, which].astype(F32)).astype(BF16)

    def overlap(panel, part):
        field = waves[panel, part].astype(F32) * solved[panel, part].astype(F32)
        return jnp.sum(field, axis=0, keepdims=True)

    loads[0].wait()
    loads[1].wait()
    base[c] = matmul(rows[...], inv[...])
    pl.semaphore_wait(barrier, n - 1 + 2 * (groups - 1))

    @pl.when(top & (c == 1))
    def _():
        solved[1] = base[1].astype(BF16)

    if relay:
        @pl.when(owner & jnp.logical_not(top) & (c == 1))
        def _():
            loads[3].wait()
            mats[1, 1] = product(1)
            loads[2].wait()
            mats[1, 0] = product(0)
            down_whole(0).wait_recv()
            high = base[1] + matmul(whole[1], mats[1, 1])
            down_whole(1).wait_recv()
            high = high + matmul(whole[0, :, halves[0]], mats[1, 0, halves[0]])
            down_whole(2).wait_recv()
            onward.start()
            solved[1] = (high + matmul(whole[0, :, halves[1]], mats[1, 0, halves[1]])).astype(BF16)

    @pl.when(owner & (c == 1))
    def _():
        give_top.start()
        send_down(0)

        @pl.when(top)
        def _():
            loads[2].wait()
            loads[3].wait()

        loads[4].wait()
        mine_part[1] = overlap(1, slice(None))
        mine_part[0] = jnp.zeros_like(mine_part[0])

    @pl.when(owner & (c == 0))
    def _():
        loads[2].wait()
        mats[0, 0] = product(0)
        loads[3].wait()

        if relay:
            @pl.when(jnp.logical_not(top))
            def _():
                mats[0, 1] = product(1)
                onward.wait_recv()
                base[0] += matmul(whole[0], mats[0, 1])

        give_top.wait_recv()
        for i, cols in enumerate(halves):
            solved[0, :, cols] = (base[0, :, cols] + matmul(solved[1], mats[0, 0, :, cols])).astype(BF16)
            send_down(1 + i)
        loads[4].wait()
        mine_part[0] = overlap(0, slice(None))
        mine_part[1] = jnp.zeros_like(mine_part[1])

    @pl.when(jnp.logical_not(owner))
    def _():
        give_base.start()
        loads[3].wait()
        mats[c, 1] = product(1)
        give_mat[1].start()
        loads[2].wait()
        mats[c, 0] = product(0)
        give_mat[0].start()
        loads[4].wait()
        give_waves.start()

        take_base.wait_recv()
        take_mat[1].wait_recv()
        take_mat[0].wait_recv()
        take_waves.wait_recv()

    def solve(last):
        down(0).wait_recv()
        high = base[1, mine] + matmul(above[1], mats[1, 1])
        down(1).wait_recv()
        left = above[0, :, halves[0]]
        high = high + matmul(left, mats[1, 0, halves[0]])
        low = base[0, mine] + matmul(left, mats[0, 1, halves[0]])
        down(2).wait_recv()
        right = above[0, :, halves[1]]
        high = (high + matmul(right, mats[1, 0, halves[1]])).astype(BF16)
        solved[1, mine] = high
        if not last:
            down(0).start()
        low = low + matmul(right, mats[0, 1, halves[1]])
        for i, cols in enumerate(halves):
            piece = low[:, i * wide:(i + 1) * wide] + matmul(high, mats[0, 0, :, cols])
            solved[0, mine, cols] = piece.astype(BF16)
            if not last:
                down(1 + i).start()
        mine_part[1] = overlap(1, mine)
        mine_part[0] = overlap(0, mine)

    @pl.when(bottom & jnp.logical_not(owner))
    def _():
        solve(True)

    @pl.when(jnp.logical_not(bottom | owner))
    def _():
        solve(False)

    slot = 2 * g + c

    def part_to(step, flip):
        to = lax.rem(c + flip, 2)
        return remote(mine_part.at[to], parts.at[slot], part_send.at[2 * step + flip],
                      part_recv.at[slot], first + to, lax.rem(g + step, groups))

    def part_from(step, flip):
        owner = 2 * lax.rem(g + groups - step, groups) + lax.rem(c + flip, 2)
        return remote(mine_part.at[0], parts.at[owner], part_send.at[2 * step + flip],
                      part_recv.at[owner], peer, g)

    partners = [(step, flip) for step in range(groups) for flip in range(2) if step + flip > 0]
    for step, flip in reversed(partners):
        part_to(step, flip).start()
    parts[slot] = mine_part[c]

    @pl.when(jnp.logical_not(owner))
    def _():
        give_back.start()
        take_back.wait_recv()

    adjoint[...] = solved[c]

    for step, flip in partners:
        part_from(step, flip).wait_recv()
    grad = parts[0]
    for i in range(1, 2 * groups):
        grad = grad + parts[i]
    squares[k] = jnp.broadcast_to(jnp.sum(grad * grad, axis=1, keepdims=True), (1, 128))

    def square_copy(step, owner):
        return remote(squares.at[owner], squares.at[owner], sq_send.at[step], sq_recv.at[owner],
                      lax.rem(k + step, n), g)

    for step in reversed(range(1, n)):
        square_copy(step, k).start()
    for step in range(1, n):
        square_copy(step, lax.rem(k + n - step, n)).wait_recv()
    total = squares[0]
    for panel in range(1, n):
        total = total + squares[panel]
    count = float(n * grad.shape[1])
    scale = jnp.sqrt(total / count + 1e-06)
    direction[...] = grad / jnp.broadcast_to(scale[:, :1], grad.shape)

    for step, flip in partners:
        part_to(step, flip).wait_send()
    for step in range(1, n):
        square_copy(step, k).wait_send()

    @pl.when(owner & (c == 1))
    def _():
        give_top.wait_send()

    def sent_down(items):
        if relay:
            @pl.when(top)
            def _():
                for i in items:
                    down_whole(i).wait_send()

        if n > 2:
            @pl.when(jnp.logical_not(top) if relay else top)
            def _():
                for i in items:
                    for core in range(2):
                        down_top(i, core).wait_send()

    @pl.when(owner & (c == 1))
    def _():
        sent_down((0,))

        if relay:
            @pl.when(jnp.logical_not(top))
            def _():
                onward.wait_send()

    @pl.when(owner & (c == 0))
    def _():
        sent_down((1, 2))

    @pl.when(jnp.logical_not(owner))
    def _():
        give_base.wait_send()
        give_mat[0].wait_send()
        give_mat[1].wait_send()
        give_waves.wait_send()
        give_back.wait_send()

        @pl.when(jnp.logical_not(bottom))
        def _():
            for i in range(3):
                down(i).wait_send()


def solution(mesh):
    n = mesh.shape["chain"]
    groups = mesh.shape["src"]

    def per_device(sources, forward, inv_diag, coupling, pattern):
        count, width = sources.shape
        anywhere = pl.BlockSpec(memory_space=pl.ANY)
        adjoint, direction = pl.pallas_call(
            functools.partial(kernel, n, groups),
            out_shape=(
                pltpu.VMEM((count, width), BF16),
                pltpu.VMEM((1, width), F32),
            ),
            in_specs=[pl.BlockSpec(memory_space=pltpu.SMEM)] + [anywhere] * 4,
            out_specs=(pl.BlockSpec(memory_space=pltpu.VMEM),) * 2,
            scratch_shapes=[
                pltpu.VMEM((count, width), BF16),
                pltpu.VMEM((2, count, width), BF16),
                pltpu.VMEM((width, width), BF16),
                pltpu.VMEM((2, width, width), BF16),
                pltpu.VMEM((2, count, width), F32),
                pltpu.VMEM((2, 2, width, width), BF16),
                pltpu.VMEM((2, count // 2, width), BF16),
                pltpu.VMEM((2, count, width), BF16),
                pltpu.VMEM((2, count, width), BF16),
                pltpu.VMEM((2, 1, width), F32),
                pltpu.VMEM((2 * groups, 1, width), F32),
                pltpu.VMEM((n, 1, 128), F32),
                pltpu.SemaphoreType.DMA((5,)),
                pltpu.SemaphoreType.DMA((5,)),
                pltpu.SemaphoreType.DMA((5,)),
                pltpu.SemaphoreType.DMA((4,)),
                pltpu.SemaphoreType.DMA((3,)),
                pltpu.SemaphoreType.DMA((3,)),
                pltpu.SemaphoreType.DMA,
                pltpu.SemaphoreType.DMA,
                pltpu.SemaphoreType.DMA((2 * groups,)),
                pltpu.SemaphoreType.DMA((2 * groups,)),
                pltpu.SemaphoreType.DMA((n,)),
                pltpu.SemaphoreType.DMA((n,)),
            ],
            compiler_params=pltpu.CompilerParams(
                collective_id=0, has_side_effects=True, vmem_limit_bytes=60 * 1024 * 1024
            ),
            cost_estimate=pl.CostEstimate(
                flops=2 * width * width * (2 * width + 3 * count),
                bytes_accessed=6 * width * width + 6 * count * width,
                transcendentals=0,
            ),
        )(pattern, sources, forward, inv_diag, coupling)
        return adjoint, direction.reshape(width)

    return jax.shard_map(
        per_device,
        mesh=mesh,
        in_specs=(
            P("src", "chain"),
            P("src", "chain"),
            P("chain", None, None),
            P("chain", None, None, None),
            P("chain", None),
        ),
        out_specs=(P("src", "chain"), P("chain")),
        check_vma=False,
    )
```

```python
import functools

import jax
import jax.numpy as jnp
from jax import lax
from jax.experimental import pallas as pl
from jax.experimental.pallas import tpu as pltpu
from jax.sharding import PartitionSpec as P

F32 = jnp.float32
BF16 = jnp.bfloat16
MESH = pl.DeviceIdType.MESH


def matmul(a, b):
    return jnp.dot(a, b, preferred_element_type=F32)


def kernel(n, groups, pattern, sources, forward, inv_diag, coupling, adjoint, direction,
           rows, waves, inv, blocks, base, mats, above, solved, mine_part, parts, squares,
           load_sem, pair_send, pair_recv, down_send, down_recv, back_send, back_recv,
           part_send, part_recv, sq_send, sq_recv):
    k = lax.axis_index("chain")
    g = lax.axis_index("src")
    c = lax.rem(k, 2)
    first = k - c
    peer = first + 1 - c
    top = k >= n - 2
    bottom = k < 2
    half = rows.shape[0] // 2
    mine = pl.ds(pl.multiple_of(c * half, half), half)
    theirs = pl.ds(pl.multiple_of((1 - c) * half, half), half)

    loads = [
        pltpu.make_async_copy(inv_diag.at[0], inv, load_sem.at[0]),
        pltpu.make_async_copy(sources, rows, load_sem.at[1]),
        pltpu.make_async_copy(coupling.at[0, 0], blocks.at[0], load_sem.at[2]),
        pltpu.make_async_copy(coupling.at[0, 1], blocks.at[1], load_sem.at[3]),
        pltpu.make_async_copy(forward, waves.at[c], load_sem.at[4]),
    ]
    barrier = pltpu.get_barrier_semaphore()
    for step in range(1, n):
        pl.semaphore_signal(barrier, inc=1, device_id=(lax.rem(k + step, n), g), device_id_type=MESH)
    for step in range(1, groups):
        for other in (k, peer):
            pl.semaphore_signal(barrier, inc=1, device_id=(other, lax.rem(g + step, groups)), device_id_type=MESH)

    for i in (0, 1, 3, 2, 4):
        loads[i].start()

    def remote(src, dst, send, recv, chain_to, src_to):
        return pltpu.make_async_remote_copy(
            src_ref=src, dst_ref=dst, send_sem=send, recv_sem=recv,
            device_id=(chain_to, src_to), device_id_type=MESH,
        )

    def pair(i, ref):
        return remote(ref, ref, pair_send.at[i], pair_recv.at[i], peer, g)

    give_base = pair(0, base.at[c, theirs])
    take_base = pair(0, base.at[1 - c, mine])
    give_mat = [pair(1, mats.at[c, 0]), pair(2, mats.at[c, 1])]
    take_mat = [pair(1, mats.at[1 - c, 0]), pair(2, mats.at[1 - c, 1])]
    give_waves = pair(3, waves.at[c, theirs])
    take_waves = pair(3, waves.at[1 - c, mine])
    give_top = pair(4, solved.at[1])
    give_back = remote(solved.at[1 - c, mine], solved.at[1 - c, mine], back_send, back_recv, peer, g)
    take_back = remote(solved.at[c, theirs], solved.at[c, theirs], back_send, back_recv, peer, g)

    wide = rows.shape[1] // 2
    halves = (pl.ds(0, wide), pl.ds(wide, wide))

    def down(i):
        if i == 0:
            src, dst = solved.at[1, mine], above.at[1]
        else:
            src, dst = solved.at[0, mine, halves[i - 1]], above.at[0, :, halves[i - 1]]
        return remote(src, dst, down_send.at[i], down_recv.at[i], lax.max(k - 2, 0), g)

    def down_top(i, core):
        part = pl.ds(core * half, half)
        if i == 0:
            src, dst, sent = solved.at[1, part], above.at[1], core
        else:
            src, dst = solved.at[0, part, halves[i - 1]], above.at[0, :, halves[i - 1]]
            sent = 2 * (i - 1) + core
        return remote(src, dst, down_send.at[sent], down_recv.at[i], lax.max(first - 2 + core, 0), g)

    def product(which):
        return (matmul(blocks[which], inv[...]) * -pattern[0, which].astype(F32)).astype(BF16)

    def overlap(panel, part):
        field = waves[panel, part].astype(F32) * solved[panel, part].astype(F32)
        return jnp.sum(field, axis=0, keepdims=True)

    loads[0].wait()
    loads[1].wait()
    base[c] = matmul(rows[...], inv[...])
    pl.semaphore_wait(barrier, n - 1 + 2 * (groups - 1))

    @pl.when(top & (c == 1))
    def _():
        solved[1] = base[1].astype(BF16)
        give_top.start()
        if n > 2:
            for core in range(2):
                down_top(0, core).start()
        loads[2].wait()
        loads[3].wait()
        loads[4].wait()
        mine_part[1] = overlap(1, slice(None))
        mine_part[0] = jnp.zeros_like(mine_part[0])

    @pl.when(top & (c == 0))
    def _():
        loads[2].wait()
        mats[0, 0] = product(0)
        give_top.wait_recv()
        for i, cols in enumerate(halves):
            solved[0, :, cols] = (base[0, :, cols] + matmul(solved[1], mats[0, 0, :, cols])).astype(BF16)
            if n > 2:
                for core in range(2):
                    down_top(1 + i, core).start()
        loads[3].wait()
        loads[4].wait()
        mine_part[0] = overlap(0, slice(None))
        mine_part[1] = jnp.zeros_like(mine_part[1])

    @pl.when(jnp.logical_not(top))
    def _():
        give_base.start()
        loads[3].wait()
        mats[c, 1] = product(1)
        give_mat[1].start()
        loads[2].wait()
        mats[c, 0] = product(0)
        give_mat[0].start()
        loads[4].wait()
        give_waves.start()

        take_base.wait_recv()
        take_mat[1].wait_recv()
        take_mat[0].wait_recv()
        take_waves.wait_recv()

    def solve(last):
        down(0).wait_recv()
        high = base[1, mine] + matmul(above[1], mats[1, 1])
        down(1).wait_recv()
        left = above[0, :, halves[0]]
        high = high + matmul(left, mats[1, 0, halves[0]])
        low = base[0, mine] + matmul(left, mats[0, 1, halves[0]])
        down(2).wait_recv()
        right = above[0, :, halves[1]]
        high = (high + matmul(right, mats[1, 0, halves[1]])).astype(BF16)
        solved[1, mine] = high
        if not last:
            down(0).start()
        low = low + matmul(right, mats[0, 1, halves[1]])
        for i, cols in enumerate(halves):
            piece = low[:, i * wide:(i + 1) * wide] + matmul(high, mats[0, 0, :, cols])
            solved[0, mine, cols] = piece.astype(BF16)
            if not last:
                down(1 + i).start()
        mine_part[1] = overlap(1, mine)
        mine_part[0] = overlap(0, mine)

    @pl.when(bottom & jnp.logical_not(top))
    def _():
        solve(True)

    @pl.when(jnp.logical_not(bottom | top))
    def _():
        solve(False)

    slot = 2 * g + c

    def part_to(step, flip):
        to = lax.rem(c + flip, 2)
        return remote(mine_part.at[to], parts.at[slot], part_send.at[2 * step + flip],
                      part_recv.at[slot], first + to, lax.rem(g + step, groups))

    def part_from(step, flip):
        owner = 2 * lax.rem(g + groups - step, groups) + lax.rem(c + flip, 2)
        return remote(mine_part.at[0], parts.at[owner], part_send.at[2 * step + flip],
                      part_recv.at[owner], peer, g)

    partners = [(step, flip) for step in range(groups) for flip in range(2) if step + flip > 0]
    for step, flip in reversed(partners):
        part_to(step, flip).start()
    parts[slot] = mine_part[c]

    @pl.when(jnp.logical_not(top))
    def _():
        give_back.start()

    for step, flip in partners:
        part_from(step, flip).wait_recv()
    grad = parts[0]
    for i in range(1, 2 * groups):
        grad = grad + parts[i]
    squares[k] = jnp.broadcast_to(jnp.sum(grad * grad, axis=1, keepdims=True), (1, 128))

    def square_copy(step, owner):
        return remote(squares.at[owner], squares.at[owner], sq_send.at[step], sq_recv.at[owner],
                      lax.rem(k + step, n), g)

    for step in reversed(range(1, n)):
        square_copy(step, k).start()

    @pl.when(jnp.logical_not(top))
    def _():
        take_back.wait_recv()

    adjoint[...] = solved[c]
    for step in range(1, n):
        square_copy(step, lax.rem(k + n - step, n)).wait_recv()
    total = squares[0]
    for panel in range(1, n):
        total = total + squares[panel]
    count = float(n * grad.shape[1])
    scale = jnp.sqrt(total / count + 1e-06)
    direction[...] = grad / jnp.broadcast_to(scale[:, :1], grad.shape)

    for step, flip in partners:
        part_to(step, flip).wait_send()
    for step in range(1, n):
        square_copy(step, k).wait_send()

    @pl.when(top & (c == 1))
    def _():
        give_top.wait_send()

    if n > 2:
        @pl.when(top & (c == 1))
        def _():
            for core in range(2):
                down_top(0, core).wait_send()

        @pl.when(top & (c == 0))
        def _():
            for core in range(2):
                down_top(1, core).wait_send()
                down_top(2, core).wait_send()

    @pl.when(jnp.logical_not(top))
    def _():
        give_base.wait_send()
        give_mat[0].wait_send()
        give_mat[1].wait_send()
        give_waves.wait_send()
        give_back.wait_send()

        @pl.when(jnp.logical_not(bottom))
        def _():
            for i in range(3):
                down(i).wait_send()


def solution(mesh):
    n = mesh.shape["chain"]
    groups = mesh.shape["src"]

    def per_device(sources, forward, inv_diag, coupling, pattern):
        count, width = sources.shape
        anywhere = pl.BlockSpec(memory_space=pl.ANY)
        adjoint, direction = pl.pallas_call(
            functools.partial(kernel, n, groups),
            out_shape=(
                pltpu.VMEM((count, width), BF16),
                pltpu.VMEM((1, width), F32),
            ),
            in_specs=[pl.BlockSpec(memory_space=pltpu.SMEM)] + [anywhere] * 4,
            out_specs=(pl.BlockSpec(memory_space=pltpu.VMEM),) * 2,
            scratch_shapes=[
                pltpu.VMEM((count, width), BF16),
                pltpu.VMEM((2, count, width), BF16),
                pltpu.VMEM((width, width), BF16),
                pltpu.VMEM((2, width, width), BF16),
                pltpu.VMEM((2, count, width), F32),
                pltpu.VMEM((2, 2, width, width), BF16),
                pltpu.VMEM((2, count // 2, width), BF16),
                pltpu.VMEM((2, count, width), BF16),
                pltpu.VMEM((2, 1, width), F32),
                pltpu.VMEM((2 * groups, 1, width), F32),
                pltpu.VMEM((n, 1, 128), F32),
                pltpu.SemaphoreType.DMA((5,)),
                pltpu.SemaphoreType.DMA((5,)),
                pltpu.SemaphoreType.DMA((5,)),
                pltpu.SemaphoreType.DMA((4,)),
                pltpu.SemaphoreType.DMA((3,)),
                pltpu.SemaphoreType.DMA,
                pltpu.SemaphoreType.DMA,
                pltpu.SemaphoreType.DMA((2 * groups,)),
                pltpu.SemaphoreType.DMA((2 * groups,)),
                pltpu.SemaphoreType.DMA((n,)),
                pltpu.SemaphoreType.DMA((n,)),
            ],
            compiler_params=pltpu.CompilerParams(
                collective_id=0, has_side_effects=True, vmem_limit_bytes=60 * 1024 * 1024
            ),
            cost_estimate=pl.CostEstimate(
                flops=2 * width * width * (2 * width + 3 * count),
                bytes_accessed=6 * width * width + 6 * count * width,
                transcendentals=0,
            ),
        )(pattern, sources, forward, inv_diag, coupling)
        return adjoint, direction.reshape(width)

    return jax.shard_map(
        per_device,
        mesh=mesh,
        in_specs=(
            P("src", "chain"),
            P("src", "chain"),
            P("chain", None, None),
            P("chain", None, None, None),
            P("chain", None),
        ),
        out_specs=(P("src", "chain"), P("chain")),
        check_vma=False,
    )
```
